256 devices in a mesh: sector: 16 (over x_lo, z), band: 16 (over x_hi, y, core).
Axes of the slice: x: 4 (x_hi: 2, x_lo: 2; x = x_hi * 2 + x_lo), y: 4, z: 8, core: 2. Of those that a mesh axis runs over, the one named last changes fastest.
Arguments:
- queries: bfloat16 [256, 1024, 256], P('sector', 'band'), may hold values from -6 to 6
- norm_gain: float32 [256], replicated, may hold values from 0.5 to 1.5
- w_query: bfloat16 [256, 256], replicated, may hold values from -0.375 to 0.375
- w_key: bfloat16 [256, 256], replicated, may hold values from -0.375 to 0.375
- w_value: bfloat16 [256, 256], replicated, may hold values from -0.375 to 0.375
- w_out: bfloat16 [256, 256], replicated, may hold values from -0.375 to 0.375
- features: bfloat16 [131072, 256], P(('sector', 'band')), may hold values from -160 to 160
- visible: int32 [256, 1024, 3], P('sector', 'band'), may hold values from 0 to 3071, as said below
- live: int32 [256, 1024, 3], P('sector', 'band'), may hold values from 0 to 1, as said below
Outputs:
- attended: bfloat16 [256, 1024, 256], P('sector', 'band')
The draws below stay inside these ranges and needn't reach their ends.
Inputs may be any that keep to these rules, and one draw needn't show every extreme that they name: `visible`: on each device (s, j), the 3072 entries name every code from 0 to 3071 exactly once. `live`: 1 marks an entry that contributes, 0 one that does not.
All inputs are finite; a program needn't handle non-finite values.
Results may differ from the reference program's by a relative error of at most 0.0025.
The reference program's roundings to bfloat16 on the way count: a program that leaves them out, or rounds other values in their place, can miss the bound.
Values may be sent and summed in bfloat16 or wider, within the bound.
A program may use at most 128 MiB of HBM per device.

```python
import jax
import jax.numpy as jnp
from jax import lax

D = 256
HEADS = 8
HD = 32
QA = 16
QR = 64
TOP = 3
BLK_DEV = 8
KB = 1024
CAP = 128
NSA = 256
NBR = 1024
KEYS = 131072
N_SECTOR = 16
N_BAND = 16


def draw_features(key, part):
    values_drawn = jnp.clip(jax.random.normal(key, (KEYS, D), jnp.float32), -4.0, 4.0)
    return values_drawn.astype(jnp.bfloat16)


def draw_visible(key, part):
    sectors = NSA // QA
    bands = NBR // QR
    entry_total = QA * QR * TOP
    device_keys = jax.random.split(key, sectors * bands)
    orders = jax.vmap(lambda device_key: jax.random.permutation(device_key, entry_total))(device_keys)
    orders = orders.reshape(sectors, bands, QA, QR, TOP).transpose(0, 2, 1, 3, 4)
    return orders.reshape(NSA, NBR, TOP).astype(jnp.int32)


def draw_live(key, part):
    range_index = jnp.arange(NBR, dtype=jnp.int32)
    threshold = 900 - 600 * range_index // NBR
    ticket = jax.random.randint(key, (NSA, NBR, TOP), 0, 1000)
    return (ticket < threshold[None, :, None]).astype(jnp.int32)


def steps_of(rng, extent, shards, smallest, largest):
    factor_of, own = 1.0, jax.random.fold_in(rng, 6)
    for position, shards_of in shards:
        steps = jnp.exp(jax.random.uniform(jax.random.fold_in(own, position), (shards_of,), jnp.float32, smallest / len(shards), largest / len(shards)))
        factor_of = factor_of * jnp.repeat(steps, extent[position] // shards_of).reshape([-1 if axis == position else 1 for axis in range(len(extent))])
    return factor_of


def gaussian(own_key, shape, scale, bound, cuts=(), kind=jnp.bfloat16):
    gain = steps_of(own_key, shape, cuts, -0.22, 0.18) if cuts else 1.0
    values = jax.random.normal(own_key, shape, jnp.float32) * scale * gain
    return jnp.minimum(jnp.maximum(values, -bound), bound).astype(kind)


def setup_inputs(seed: int = 0) -> dict:
    keys = jax.random.split(jax.random.key(seed), 10)
    queries = gaussian(keys[0], (NSA, NBR, D), 1.0, 6.0, ((0, 16), (1, 16)))
    norm_gain = jnp.clip(jax.random.uniform(keys[1], (D,), jnp.float32, 0.5, 1.5), 0.5, 1.5)
    w_query = gaussian(keys[2], (D, D), D ** -0.5, 0.375)
    w_key = gaussian(keys[3], (D, D), D ** -0.5, 0.375)
    w_value = gaussian(keys[4], (D, D), D ** -0.5, 0.375)
    w_out = gaussian(keys[5], (D, D), D ** -0.5, 0.375)
    features = draw_features(jax.random.fold_in(keys[9], 71), 0)
    visible = draw_visible(jax.random.fold_in(keys[9], 71), 0)
    live = draw_live(jax.random.fold_in(keys[9], 71), 0)
    return dict(queries=queries, norm_gain=norm_gain, w_query=w_query, w_key=w_key, w_value=w_value, w_out=w_out, features=features, visible=visible, live=live)


def attend(rows, block):
    row_count = rows.shape[0]
    key_count = block.shape[0]
    query_heads = rows.reshape(row_count, HEADS, HD).transpose(1, 0, 2)
    key_heads = block[:, :D].reshape(key_count, HEADS, HD).transpose(1, 0, 2)
    value_heads = block[:, D:].reshape(key_count, HEADS, HD).transpose(1, 0, 2)

    def one_head(triple):
        query_head, key_head, value_head = triple
        scores = jnp.dot(query_head, key_head.T, preferred_element_type=jnp.float32) * HD ** (-0.5)
        peak = lax.optimization_barrier(jnp.max(scores, axis=-1, keepdims=True))
        expo = jnp.exp(scores - peak)
        weights = (expo / lax.optimization_barrier(jnp.sum(expo, axis=-1, keepdims=True))).astype(jnp.bfloat16)
        return jnp.dot(weights, value_head, preferred_element_type=jnp.float32).astype(jnp.bfloat16)
    heads_out = lax.map(one_head, (query_heads, key_heads, value_heads))
    return heads_out.transpose(1, 0, 2).reshape(row_count, D)

def reference(queries, norm_gain, w_query, w_key, w_value, w_out, features, visible, live):
    sectors = N_SECTOR
    bands = N_BAND
    query_count = QA * QR
    slot_total = 3 * BLK_DEV * CAP
    values_in = queries.astype(jnp.float32)
    average = lax.optimization_barrier(jnp.mean(values_in, axis=-1, keepdims=True))
    spread = lax.optimization_barrier(jnp.mean((values_in - average) ** 2, axis=-1, keepdims=True))
    normed = ((values_in - average) * lax.rsqrt(spread + 1e-05) * norm_gain).astype(jnp.bfloat16)
    projected = jnp.dot(normed.reshape(-1, D), w_query, preferred_element_type=jnp.float32).astype(jnp.bfloat16)
    w_both = jnp.concatenate([w_key, w_value], axis=1)
    key_values = jnp.dot(features, w_both, preferred_element_type=jnp.float32).astype(jnp.bfloat16)
    key_values = key_values.reshape(sectors, BLK_DEV, KB, 2 * D)

    def per_device(array, last):
        return array.reshape(sectors, QA, bands, QR, last).transpose(0, 2, 1, 3, 4).reshape(sectors, bands, query_count * last)
    proj_dev = per_device(projected.reshape(sectors * QA, bands * QR, D), D).reshape(sectors, bands, query_count, D)
    codes_dev = per_device(visible, TOP)
    live_dev = per_device(live, TOP).reshape(sectors, bands, query_count, TOP)

    def per_sector(inputs):
        sector_index, rows, slot_codes, live_rows = inputs

        def fill(device_rows, device_codes):
            empty = jnp.zeros((slot_total, D), jnp.bfloat16)
            return empty.at[device_codes].set(jnp.repeat(device_rows, TOP, axis=0))
        buffers = jax.vmap(fill)(rows, slot_codes).reshape(bands, 3, BLK_DEV, CAP, D)
        buffers = buffers.transpose(1, 2, 0, 3, 4).reshape(3 * BLK_DEV, bands * CAP, D)
        owners = (sector_index + jnp.arange(3, dtype=jnp.int32) - 1) % sectors
        blocks = key_values[owners].reshape(3 * BLK_DEV, KB, 2 * D)
        results = lax.map(lambda pair: attend(pair[0], pair[1]), (buffers, blocks))
        results = results.reshape(3, BLK_DEV, bands, CAP, D).transpose(2, 0, 1, 3, 4).reshape(bands, slot_total, D)
        picked = jax.vmap(lambda table, device_codes: table[device_codes])(results, slot_codes)
        picked = picked.reshape(bands, query_count, TOP, D).astype(jnp.float32)
        summed = lax.optimization_barrier(jnp.sum(picked * live_rows[..., None].astype(jnp.float32), axis=2))
        return summed.astype(jnp.bfloat16)
    summed = lax.map(per_sector, (jnp.arange(sectors, dtype=jnp.int32), proj_dev, codes_dev, live_dev))
    summed = summed.reshape(sectors, bands, QA, QR, D).transpose(0, 2, 1, 3, 4).reshape(-1, D)
    final = jnp.dot(summed, w_out, preferred_element_type=jnp.float32) + queries.reshape(-1, D).astype(jnp.float32)
    return final.astype(jnp.bfloat16).reshape(sectors * QA, bands * QR, D)
```

```python
import math

import jax
import jax.numpy as jnp
from jax import lax
from jax.experimental import pallas as pl
from jax.experimental.pallas import tpu as pltpu
from jax.sharding import PartitionSpec as P

HEADS = 8
BLK_DEV = 8
CAP = 128
N_SECTOR = 16
F32 = jnp.float32
BF16 = jnp.bfloat16
MESH = pl.DeviceIdType.MESH
LANES = 128
ROWS = 64


def kernel(
    queries, norm_gain, w_query, w_key, w_value, w_out, features, visible, live, out,
    proj, code_cols, code_rows, slots, qbuf, results, table, feats, relay, k_t, v_one, acc,
    f_send, f_recv, x_send, x_recv, g_send, q_send, q_recv, r_send, r_recv,
):
    azim, ranges, width = queries.shape
    query_count = azim * ranges
    entries = visible.shape[2]
    half, keys = features.shape[0], 2 * features.shape[0]
    head_size = width // HEADS
    scale = math.log2(math.e) * head_size ** -0.5
    nh = LANES // head_size

    s, j = lax.axis_index("sector"), lax.axis_index("band")
    x, y, c = j // 8, (j // 2) % 4, j % 2
    parity = y % 2
    away = (y + c) % 2

    def band(xx, yy, cc):
        return xx * 8 + yy * 2 + cc

    def sector(offset):
        return (s + offset + N_SECTOR) % N_SECTOR

    y_up, y_down = (y + 1) % 4, (y + 3) % 4
    other = (c + 1) % 2
    x_far = (x + 1) % 2

    barrier = pltpu.get_barrier_semaphore()
    greeted = [(s, band(x, y, other)), (s, band(x_far, y, c))]
    greeted += [(s, band(x, yy, cc)) for yy in (y_up, y_down) for cc in (0, 1)]
    greeted += [(sector(o), band(x, y, cc)) for o in (-1, 1) for cc in (0, 1)]
    for device in greeted:
        pl.semaphore_signal(barrier, inc=1, device_id=device, device_id_type=MESH)

    values_in = queries[...].reshape(query_count, width).astype(F32)
    average = jnp.mean(values_in, axis=-1, keepdims=True)
    spread = jnp.mean((values_in - average) ** 2, axis=-1, keepdims=True)
    normed = ((values_in - average) * lax.rsqrt(spread + 1e-05) * norm_gain[...]).astype(BF16)
    proj[...] = jnp.dot(normed, w_query[...], preferred_element_type=F32).astype(BF16)

    def remote(src, dst, send, recv, device):
        return pltpu.make_async_remote_copy(
            src_ref=src, dst_ref=dst, send_sem=send, recv_sem=recv, device_id=device, device_id_type=MESH
        )

    def local_of(xx, yy):
        return xx * 2 + yy // 2

    def spread_copies(src, xx, row):
        li = local_of(xx, y)
        up = remote(src, feats.at[li, c], f_send.at[row, 0], f_recv.at[li, c], (s, band(x, y_up, parity)))
        down = remote(src, feats.at[li, c], f_send.at[row, 1], f_recv.at[li, c], (s, band(x, y_down, parity)))
        across = remote(src, feats.at[li, c], f_send.at[row, 2], f_recv.at[li, c], (s, band(x, y, other)))
        stay = pltpu.make_async_copy(src, feats.at[li, c], f_recv.at[li, c])
        return up, down, across, stay

    def spread_start(src, xx, row):
        up, down, across, stay = spread_copies(src, xx, row)

        @pl.when(away == 1)
        def _():
            across.start()

        @pl.when(away == 0)
        def _():
            stay.start()

        up.start()
        down.start()

    def spread_wait(src, xx, row):
        up, down, across, stay = spread_copies(src, xx, row)
        up.wait_send()
        down.wait_send()

        @pl.when(away == 1)
        def _():
            across.wait_send()

    def forward_copies(xx, row):
        low, high = local_of(xx, y_down), local_of(xx, y_up)
        up = remote(feats.at[low, 0], feats.at[low, 0], g_send.at[row, 0], f_recv.at[low, 0], (s, band(x, y_up, c)))
        down = remote(feats.at[high, 1], feats.at[high, 1], g_send.at[row, 1], f_recv.at[high, 1], (s, band(x, y_down, c)))
        return up, down

    exchange = remote(features, relay, x_send.at[0], x_recv.at[0], (s, band(x_far, y, c)))

    def step_block(k, core):
        yy = (y + (y + core) % 2 + 2 * (k % 2)) % 4
        xx = (x + k // 2) % 2
        return xx, yy

    def query_copy(k, o, d):
        core = (c + d) % 2
        xx, yy = step_block(k, core)
        b, li = xx * 4 + yy, local_of(xx, yy)
        if o == 1 and d == 0:
            return pltpu.make_async_copy(slots.at[o, b], qbuf.at[li, 2 * o + d], q_recv.at[li, 2 * o + d])
        return remote(
            slots.at[o, b], qbuf.at[li, 2 * o + d], q_send.at[k, 2 * o + d], q_recv.at[li, 2 * o + d],
            (sector(o - 1), band(x, y, core)),
        )

    def result_copy(k, o, d):
        xx, yy = step_block(k, c)
        b, li = xx * 4 + yy, local_of(xx, yy)
        if o == 1 and d == 0:
            return pltpu.make_async_copy(results.at[li, 2 * o + d], table.at[o, b], r_recv.at[o, b])
        return remote(
            results.at[li, 2 * o + d], table.at[o, b], r_send.at[k, 2 * o + d], r_recv.at[o, b],
            (sector(1 - o), band(x, y, (c + d) % 2)),
        )

    pl.semaphore_wait(barrier, len(greeted))
    exchange.start()
    spread_start(features, x, 0)

    codes = visible[...].reshape(query_count, entries).astype(F32)
    alive = live[...].reshape(query_count, entries)
    diagonal = lax.broadcasted_iota(jnp.int32, (CAP, LANES), 0) == lax.broadcasted_iota(jnp.int32, (CAP, LANES), 1)
    lived = jnp.where(alive == 1, codes, -1.0)
    for t in range(entries):
        code_cols[t] = jnp.broadcast_to(lived[:, t : t + 1], (query_count, LANES))
        spread_code = jnp.broadcast_to(codes[:, t : t + 1], (query_count, LANES))
        for n in range(query_count // LANES):
            piece = spread_code[n * LANES : (n + 1) * LANES]
            code_rows[t : t + 1, n * LANES : (n + 1) * LANES] = jnp.sum(
                jnp.where(diagonal, piece, 0.0), axis=0, keepdims=True
            )

    slot_index = lax.broadcasted_iota(jnp.int32, (CAP, query_count), 0).astype(F32)

    @pl.loop(0, 4)
    def _(k):
        for d in (0, 1):
            xx, yy = step_block(k, (c + d) % 2)
            b = xx * 4 + yy
            picks = []
            for o in range(3):
                base = ((o * BLK_DEV + b) * CAP).astype(F32)
                hit = slot_index == (code_rows[0:1, :] - base)
                for t in range(1, entries):
                    hit = hit | (slot_index == (code_rows[t : t + 1, :] - base))
                picks.append(jnp.where(hit, 1.0, 0.0).astype(BF16))
            picked = jnp.dot(jnp.concatenate(picks, axis=0), proj[...], preferred_element_type=F32).astype(BF16)
            for o in range(3):
                slots[o, b] = picked[o * CAP : (o + 1) * CAP]
            for o in (0, 2, 1):
                query_copy(k, o, d).start()

    for t in range(2):
        v_one[t, :, LANES:] = jnp.ones((keys, LANES), BF16)
    w_key_t = w_key[...].T
    head = lax.broadcasted_iota(jnp.int32, (ROWS, LANES), 1) // head_size

    @pl.loop(0, 4)
    def _(k):
        xx, yy = step_block(k, c)
        li = local_of(xx, yy)

        @pl.when((away == 1) & (k % 2 == 0))
        def _():
            for yn in (y_down, y_up):
                for h in (0, 1):
                    here = feats.at[local_of(xx, yn), h]
                    pltpu.make_async_copy(here, here, f_recv.at[local_of(xx, yn), h]).wait()
            for copy in forward_copies(xx, k // 2):
                copy.start()

        @pl.when(away == 0)
        def _():
            for h in (0, 1):
                here = feats.at[li, h]
                pltpu.make_async_copy(here, here, f_recv.at[li, h]).wait()

        @pl.when(k == 1)
        def _():
            exchange.wait_recv()
            spread_start(relay, x_far, 1)

        tokens = feats[li].reshape(keys, width)
        k_t[...] = lax.dot_general(
            w_key_t, tokens, (((1,), (1,)), ((), ())), preferred_element_type=F32
        ).astype(BF16)
        value = jnp.dot(tokens, w_value[...], preferred_element_type=F32).astype(BF16)
        for t in range(2):
            v_one[t, :, :LANES] = value[:, t * LANES : (t + 1) * LANES]

        for o in range(3):
            for d in (0, 1):
                here = qbuf.at[li, 2 * o + d]
                pltpu.make_async_copy(here, here, q_recv.at[li, 2 * o + d]).wait()

        tiles = [(src, r0, t) for src in (0, 1, 4, 5, 2, 3) for r0 in range(0, CAP, ROWS) for t in range(2)]

        def scores_of(src, r0, t):
            rows = qbuf[li, src, r0 : r0 + ROWS, t * LANES : (t + 1) * LANES]
            stacked = jnp.concatenate([jnp.where(head == h, rows, jnp.zeros((), BF16)) for h in range(nh)], axis=0)
            return jnp.dot(stacked, k_t[t * LANES : (t + 1) * LANES, :], preferred_element_type=F32)

        scores = scores_of(*tiles[0])
        for i, (src, r0, t) in enumerate(tiles):
            later = scores_of(*tiles[i + 1]) if i + 1 < len(tiles) else None
            peak = jnp.max(scores, axis=1, keepdims=True)
            expo = jnp.exp2((scores - peak) * scale).astype(BF16)
            both = jnp.dot(expo, v_one[t], preferred_element_type=F32)
            parts = both[:, :LANES] / both[:, LANES:]
            merged = parts[:ROWS]
            for h in range(1, nh):
                merged = jnp.where(head == h, parts[h * ROWS : (h + 1) * ROWS], merged)
            results[li, src, r0 : r0 + ROWS, t * LANES : (t + 1) * LANES] = merged.astype(BF16)
            scores = later

        for o in (0, 2, 1):
            for d in (1, 0):
                result_copy(k, o, d).start()

    lane_index = lax.broadcasted_iota(jnp.int32, (query_count, LANES), 1).astype(F32)

    @pl.loop(0, 4)
    def _(k):
        masks, rows = [], []
        for d in (0, 1):
            xx, yy = step_block(k, (c + d) % 2)
            b = xx * 4 + yy
            for o in range(3):
                here = table.at[o, b]
                pltpu.make_async_copy(here, here, r_recv.at[o, b]).wait()
                target = lane_index + ((o * BLK_DEV + b) * CAP).astype(F32)
                hit = code_cols[0] == target
                for t in range(1, entries):
                    hit = hit | (code_cols[t] == target)
                masks.append(jnp.where(hit, 1.0, 0.0).astype(BF16))
                rows.append(table[o, b])
        part = jnp.dot(jnp.concatenate(masks, axis=1), jnp.concatenate(rows, axis=0), preferred_element_type=F32)

        @pl.when(k == 0)
        def _():
            acc[...] = part

        @pl.when(k > 0)
        def _():
            acc[...] += part

    summed = acc[...].astype(BF16)
    final = jnp.dot(summed, w_out[...], preferred_element_type=F32) + queries[...].reshape(query_count, width).astype(F32)
    out[...] = final.astype(BF16).reshape(azim, ranges, width)

    exchange.wait_send()
    spread_wait(features, x, 0)
    spread_wait(relay, x_far, 1)

    @pl.when(away == 1)
    def _():
        for row, xx in enumerate((x, x_far)):
            for copy in forward_copies(xx, row):
                copy.wait_send()

    @pl.loop(0, 4)
    def _(k):
        for o in range(3):
            for d in (0, 1):
                if not (o == 1 and d == 0):
                    query_copy(k, o, d).wait_send()
                    result_copy(k, o, d).wait_send()


def shards(queries, norm_gain, w_query, w_key, w_value, w_out, features, visible, live):
    azim, ranges, width = queries.shape
    query_count = azim * ranges
    half, keys = features.shape[0], 2 * features.shape[0]
    entries = visible.shape[2]
    dma = pltpu.SemaphoreType.DMA
    return pl.pallas_call(
        kernel,
        out_shape=jax.ShapeDtypeStruct(queries.shape, BF16),
        in_specs=[pl.BlockSpec(memory_space=pltpu.VMEM)] * 9,
        out_specs=pl.BlockSpec(memory_space=pltpu.VMEM),
        scratch_shapes=[
            pltpu.VMEM((query_count, width), BF16),
            pltpu.VMEM((entries, query_count, LANES), F32),
            pltpu.VMEM((8, query_count), F32),
            pltpu.VMEM((3, BLK_DEV, CAP, width), BF16),
            pltpu.VMEM((4, 6, CAP, width), BF16),
            pltpu.VMEM((4, 6, CAP, width), BF16),
            pltpu.VMEM((3, BLK_DEV, CAP, width), BF16),
            pltpu.VMEM((4, 2, half, width), BF16),
            pltpu.VMEM((half, width), BF16),
            pltpu.VMEM((width, keys), BF16),
            pltpu.VMEM((2, keys, 2 * LANES), BF16),
            pltpu.VMEM((query_count, width), F32),
            dma((2, 3)), dma((4, 2)), dma((1,)), dma((1,)), dma((2, 2)),
            dma((4, 6)), dma((4, 6)), dma((4, 6)), dma((3, BLK_DEV)),
        ],
        compiler_params=pltpu.CompilerParams(
            collective_id=0, has_side_effects=True, vmem_limit_bytes=56 * 2**20
        ),
    )(queries, norm_gain.reshape(1, -1), w_query, w_key, w_value, w_out, features, visible, live)


def solution(mesh):
    return jax.shard_map(
        shards,
        mesh=mesh,
        in_specs=(
            P("sector", "band", None), P(), P(), P(), P(), P(),
            P(("sector", "band"), None),
            P("sector", "band", None), P("sector", "band", None),
        ),
        out_specs=P("sector", "band", None),
        check_vma=False,
    )
```

```python
import math

import jax
import jax.numpy as jnp
from jax import lax
from jax.experimental import pallas as pl
from jax.experimental.pallas import tpu as pltpu
from jax.sharding import PartitionSpec as P

HEADS = 8
BLK_DEV = 8
CAP = 128
N_SECTOR = 16
F32 = jnp.float32
BF16 = jnp.bfloat16
MESH = pl.DeviceIdType.MESH
LANES = 128
ROWS = 64


def kernel(
    queries, norm_gain, w_query, w_key, w_value, w_out, features, visible, live, out,
    proj, code_cols, code_rows, slots, qbuf, results, table, feats, relay, k_t, v_all, acc,
    f_send, f_recv, x_send, x_recv, g_send, q_send, q_recv, r_send, r_recv,
):
    azim, ranges, width = queries.shape
    query_count = azim * ranges
    entries = visible.shape[2]
    half, keys = features.shape[0], 2 * features.shape[0]
    head_size = width // HEADS
    scale = math.log2(math.e) * head_size ** -0.5
    nh = LANES // head_size

    s, j = lax.axis_index("sector"), lax.axis_index("band")
    x, y, c = j // 8, (j // 2) % 4, j % 2
    parity = y % 2
    away = (y + c) % 2

    def band(xx, yy, cc):
        return xx * 8 + yy * 2 + cc

    def sector(offset):
        return (s + offset + N_SECTOR) % N_SECTOR

    y_up, y_down = (y + 1) % 4, (y + 3) % 4
    other = (c + 1) % 2
    x_far = (x + 1) % 2

    barrier = pltpu.get_barrier_semaphore()
    greeted = [(s, band(x, y, other)), (s, band(x_far, y, c))]
    greeted += [(s, band(x, yy, cc)) for yy in (y_up, y_down) for cc in (0, 1)]
    greeted += [(sector(o), band(x, y, cc)) for o in (-1, 1) for cc in (0, 1)]
    for device in greeted:
        pl.semaphore_signal(barrier, inc=1, device_id=device, device_id_type=MESH)

    values_in = queries[...].reshape(query_count, width).astype(F32)
    average = jnp.mean(values_in, axis=-1, keepdims=True)
    spread = jnp.mean((values_in - average) ** 2, axis=-1, keepdims=True)
    normed = ((values_in - average) * lax.rsqrt(spread + 1e-05) * norm_gain[...]).astype(BF16)
    proj[...] = jnp.dot(normed, w_query[...], preferred_element_type=F32).astype(BF16)

    def remote(src, dst, send, recv, device):
        return pltpu.make_async_remote_copy(
            src_ref=src, dst_ref=dst, send_sem=send, recv_sem=recv, device_id=device, device_id_type=MESH
        )

    def local_of(xx, yy):
        return xx * 2 + yy // 2

    def spread_copies(src, xx, row):
        li = local_of(xx, y)
        up = remote(src, feats.at[li, c], f_send.at[row, 0], f_recv.at[li, c], (s, band(x, y_up, parity)))
        down = remote(src, feats.at[li, c], f_send.at[row, 1], f_recv.at[li, c], (s, band(x, y_down, parity)))
        across = remote(src, feats.at[li, c], f_send.at[row, 2], f_recv.at[li, c], (s, band(x, y, other)))
        stay = pltpu.make_async_copy(src, feats.at[li, c], f_recv.at[li, c])
        return up, down, across, stay

    def spread_start(src, xx, row):
        up, down, across, stay = spread_copies(src, xx, row)

        @pl.when(away == 1)
        def _():
            across.start()

        @pl.when(away == 0)
        def _():
            stay.start()

        up.start()
        down.start()

    def spread_wait(src, xx, row):
        up, down, across, stay = spread_copies(src, xx, row)
        up.wait_send()
        down.wait_send()

        @pl.when(away == 1)
        def _():
            across.wait_send()

    def forward_copies(xx, row):
        low, high = local_of(xx, y_down), local_of(xx, y_up)
        up = remote(feats.at[low, 0], feats.at[low, 0], g_send.at[row, 0], f_recv.at[low, 0], (s, band(x, y_up, c)))
        down = remote(feats.at[high, 1], feats.at[high, 1], g_send.at[row, 1], f_recv.at[high, 1], (s, band(x, y_down, c)))
        return up, down

    exchange = remote(features, relay, x_send.at[0], x_recv.at[0], (s, band(x_far, y, c)))

    def step_block(k, core):
        yy = (y + (y + core) % 2 + 2 * (k % 2)) % 4
        xx = (x + k // 2) % 2
        return xx, yy

    def query_copy(k, o, d):
        core = (c + d) % 2
        xx, yy = step_block(k, core)
        b, li = xx * 4 + yy, local_of(xx, yy)
        if o == 1 and d == 0:
            return pltpu.make_async_copy(slots.at[o, b], qbuf.at[li, 2 * o + d], q_recv.at[li, 2 * o + d])
        return remote(
            slots.at[o, b], qbuf.at[li, 2 * o + d], q_send.at[k, 2 * o + d], q_recv.at[li, 2 * o + d],
            (sector(o - 1), band(x, y, core)),
        )

    def result_copy(k, o, d):
        xx, yy = step_block(k, c)
        b, li = xx * 4 + yy, local_of(xx, yy)
        if o == 1 and d == 0:
            return pltpu.make_async_copy(results.at[li, 2 * o + d], table.at[o, b], r_recv.at[o, b])
        return remote(
            results.at[li, 2 * o + d], table.at[o, b], r_send.at[k, 2 * o + d], r_recv.at[o, b],
            (sector(1 - o), band(x, y, (c + d) % 2)),
        )

    pl.semaphore_wait(barrier, len(greeted))
    exchange.start()
    spread_start(features, x, 0)

    codes = visible[...].reshape(query_count, entries).astype(F32)
    alive = live[...].reshape(query_count, entries)
    diagonal = lax.broadcasted_iota(jnp.int32, (CAP, LANES), 0) == lax.broadcasted_iota(jnp.int32, (CAP, LANES), 1)
    lived = jnp.where(alive == 1, codes, -1.0)
    for t in range(entries):
        code_cols[t] = jnp.broadcast_to(lived[:, t : t + 1], (query_count, LANES))
        spread_code = jnp.broadcast_to(codes[:, t : t + 1], (query_count, LANES))
        for n in range(query_count // LANES):
            piece = spread_code[n * LANES : (n + 1) * LANES]
            code_rows[t : t + 1, n * LANES : (n + 1) * LANES] = jnp.sum(
                jnp.where(diagonal, piece, 0.0), axis=0, keepdims=True
            )

    slot_index = lax.broadcasted_iota(jnp.int32, (CAP, query_count), 0).astype(F32)

    @pl.loop(0, 4)
    def _(k):
        for d in (0, 1):
            xx, yy = step_block(k, (c + d) % 2)
            b = xx * 4 + yy
            picks = []
            for o in range(3):
                base = ((o * BLK_DEV + b) * CAP).astype(F32)
                hit = slot_index == (code_rows[0:1, :] - base)
                for t in range(1, entries):
                    hit = hit | (slot_index == (code_rows[t : t + 1, :] - base))
                picks.append(jnp.where(hit, 1.0, 0.0).astype(BF16))
            picked = jnp.dot(jnp.concatenate(picks, axis=0), proj[...], preferred_element_type=F32).astype(BF16)
            for o in range(3):
                slots[o, b] = picked[o * CAP : (o + 1) * CAP]
            for o in (0, 2, 1):
                query_copy(k, o, d).start()

    w_key_t = w_key[...].T
    head = lax.broadcasted_iota(jnp.int32, (ROWS, LANES), 1) // head_size

    @pl.loop(0, 4)
    def _(k):
        xx, yy = step_block(k, c)
        li = local_of(xx, yy)

        @pl.when((away == 1) & (k % 2 == 0))
        def _():
            for yn in (y_down, y_up):
                for h in (0, 1):
                    here = feats.at[local_of(xx, yn), h]
                    pltpu.make_async_copy(here, here, f_recv.at[local_of(xx, yn), h]).wait()
            for copy in forward_copies(xx, k // 2):
                copy.start()

        @pl.when(away == 0)
        def _():
            for h in (0, 1):
                here = feats.at[li, h]
                pltpu.make_async_copy(here, here, f_recv.at[li, h]).wait()

        @pl.when(k == 1)
        def _():
            exchange.wait_recv()
            spread_start(relay, x_far, 1)

        tokens = feats[li].reshape(keys, width)
        k_t[...] = lax.dot_general(
            w_key_t, tokens, (((1,), (1,)), ((), ())), preferred_element_type=F32
        ).astype(BF16)
        v_all[...] = jnp.dot(tokens, w_value[...], preferred_element_type=F32).astype(BF16)

        for o in range(3):
            for d in (0, 1):
                here = qbuf.at[li, 2 * o + d]
                pltpu.make_async_copy(here, here, q_recv.at[li, 2 * o + d]).wait()

        tiles = [(src, r0, t) for src in (0, 1, 4, 5, 2, 3) for r0 in range(0, CAP, ROWS) for t in range(2)]

        def scores_of(src, r0, t):
            rows = qbuf[li, src, r0 : r0 + ROWS, t * LANES : (t + 1) * LANES]
            stacked = jnp.concatenate([jnp.where(head == h, rows, jnp.zeros((), BF16)) for h in range(nh)], axis=0)
            return jnp.dot(stacked, k_t[t * LANES : (t + 1) * LANES, :], preferred_element_type=F32)

        def weights_of(scores):
            peak = jnp.max(scores, axis=1, keepdims=True)
            chunk = keys // 4
            expos = [jnp.exp2((scores[:, n * chunk : (n + 1) * chunk] - peak) * scale) for n in range(4)]
            total = jnp.sum((expos[0] + expos[1]) + (expos[2] + expos[3]), axis=1, keepdims=True)
            inverse = 1.0 / total
            return jnp.concatenate([(expo * inverse).astype(BF16) for expo in expos], axis=1)

        def finish(src, r0, t, weights):
            parts = jnp.dot(weights, v_all[...], preferred_element_type=F32)[:, t * LANES : (t + 1) * LANES]
            merged = parts[:ROWS]
            for h in range(1, nh):
                merged = jnp.where(head == h, parts[h * ROWS : (h + 1) * ROWS], merged)
            results[li, src, r0 : r0 + ROWS, t * LANES : (t + 1) * LANES] = merged.astype(BF16)

        scores, weights = scores_of(*tiles[0]), None
        for i, (src, r0, t) in enumerate(tiles):
            later = scores_of(*tiles[i + 1]) if i + 1 < len(tiles) else None
            new_weights = weights_of(scores)
            if i > 0:
                finish(*tiles[i - 1], weights)
            scores, weights = later, new_weights
        finish(*tiles[-1], weights)

        for o in (0, 2, 1):
            for d in (1, 0):
                result_copy(k, o, d).start()

    lane_index = lax.broadcasted_iota(jnp.int32, (query_count, LANES), 1).astype(F32)

    @pl.loop(0, 4)
    def _(k):
        masks, rows = [], []
        for d in (0, 1):
            xx, yy = step_block(k, (c + d) % 2)
            b = xx * 4 + yy
            for o in range(3):
                here = table.at[o, b]
                pltpu.make_async_copy(here, here, r_recv.at[o, b]).wait()
                target = lane_index + ((o * BLK_DEV + b) * CAP).astype(F32)
                hit = code_cols[0] == target
                for t in range(1, entries):
                    hit = hit | (code_cols[t] == target)
                masks.append(jnp.where(hit, 1.0, 0.0).astype(BF16))
                rows.append(table[o, b])
        part = jnp.dot(jnp.concatenate(masks, axis=1), jnp.concatenate(rows, axis=0), preferred_element_type=F32)

        @pl.when(k == 0)
        def _():
            acc[...] = part

        @pl.when(k > 0)
        def _():
            acc[...] += part

    summed = acc[...].astype(BF16)
    final = jnp.dot(summed, w_out[...], preferred_element_type=F32) + queries[...].reshape(query_count, width).astype(F32)
    out[...] = final.astype(BF16).reshape(azim, ranges, width)

    exchange.wait_send()
    spread_wait(features, x, 0)
    spread_wait(relay, x_far, 1)

    @pl.when(away == 1)
    def _():
        for row, xx in enumerate((x, x_far)):
            for copy in forward_copies(xx, row):
                copy.wait_send()

    @pl.loop(0, 4)
    def _(k):
        for o in range(3):
            for d in (0, 1):
                if not (o == 1 and d == 0):
                    query_copy(k, o, d).wait_send()
                    result_copy(k, o, d).wait_send()


def shards(queries, norm_gain, w_query, w_key, w_value, w_out, features, visible, live):
    azim, ranges, width = queries.shape
    query_count = azim * ranges
    half, keys = features.shape[0], 2 * features.shape[0]
    entries = visible.shape[2]
    dma = pltpu.SemaphoreType.DMA
    return pl.pallas_call(
        kernel,
        out_shape=jax.ShapeDtypeStruct(queries.shape, BF16),
        in_specs=[pl.BlockSpec(memory_space=pltpu.VMEM)] * 9,
        out_specs=pl.BlockSpec(memory_space=pltpu.VMEM),
        scratch_shapes=[
            pltpu.VMEM((query_count, width), BF16),
            pltpu.VMEM((entries, query_count, LANES), F32),
            pltpu.VMEM((8, query_count), F32),
            pltpu.VMEM((3, BLK_DEV, CAP, width), BF16),
            pltpu.VMEM((4, 6, CAP, width), BF16),
            pltpu.VMEM((4, 6, CAP, width), BF16),
            pltpu.VMEM((3, BLK_DEV, CAP, width), BF16),
            pltpu.VMEM((4, 2, half, width), BF16),
            pltpu.VMEM((half, width), BF16),
            pltpu.VMEM((width, keys), BF16),
            pltpu.VMEM((keys, width), BF16),
            pltpu.VMEM((query_count, width), F32),
            dma((2, 3)), dma((4, 2)), dma((1,)), dma((1,)), dma((2, 2)),
            dma((4, 6)), dma((4, 6)), dma((4, 6)), dma((3, BLK_DEV)),
        ],
        compiler_params=pltpu.CompilerParams(
            collective_id=0, has_side_effects=True, vmem_limit_bytes=56 * 2**20
        ),
    )(queries, norm_gain.reshape(1, -1), w_query, w_key, w_value, w_out, features, visible, live)


def solution(mesh):
    return jax.shard_map(
        shards,
        mesh=mesh,
        in_specs=(
            P("sector", "band", None), P(), P(), P(), P(), P(),
            P(("sector", "band"), None),
            P("sector", "band", None), P("sector", "band", None),
        ),
        out_specs=P("sector", "band", None),
        check_vma=False,
    )
```
